256 devices in a mesh: section: 32 (over y, z), dp: 2 (over x_lo), tensor: 4 (over x_hi, core).
Axes of the slice: x: 4 (x_hi: 2, x_lo: 2; x = x_hi * 2 + x_lo), y: 4, z: 8, core: 2. Of those that a mesh axis runs over, the one named last changes fastest.
Arguments:
- inputs: bfloat16 [32, 2, 256, 3584], P('section', 'dp', None, 'tensor'), may hold values from -8 to 8
- qkv_weight: bfloat16 [32, 3, 3584, 3584], P('section', None, 'dp', 'tensor')
- norm_gain: bfloat16 [32, 3584], P('section'), may hold values from 0.25 to 1.75
- preempted: int32 [32], P('section'), may hold values 0 or 1
Outputs:
- outputs: bfloat16 [32, 2, 256, 3584], P('section', 'dp', None, 'tensor')
The draws below stay inside these ranges and needn't reach their ends.
All inputs are finite; a program needn't handle non-finite values. No bound on the sum of `preempted` on one device may be relied on, other than what follows from the above.
Results may differ from the reference program's by a relative error of at most 0.008.
Values may be sent and summed in bfloat16 or wider, within the bound.
A program may use at most 64 MiB of HBM per device.

```python
import math
import jax
import jax.numpy as jnp
from jax import lax

HEADS = 28
HD = 128
D = 3584
LEN = 256
SEQS = 2
SECTIONS = 32


def draw_inputs(key, part):
    key = jax.random.fold_in(key, 11)
    full_shape = (SECTIONS, SEQS, LEN, D)
    return jnp.clip(jax.random.normal(key, full_shape, jnp.float32), -6.0, 6.0).astype(jnp.bfloat16)


def draw_qkv_weight(key, part):
    key = jax.random.fold_in(key, 23)
    fan_scale = 1.0 / math.sqrt(D)

    def one_section(section_index):
        section_key = jax.random.fold_in(key, section_index)
        key_first = jax.random.fold_in(section_key, 0)
        return jnp.clip(jax.random.normal(key_first, (3, D, D), jnp.float32), -6.0, 6.0) * fan_scale
    return lax.map(one_section, jnp.arange(SECTIONS)).astype(jnp.bfloat16)


def plant(entries, rng, least, top_value):
    longest = entries.shape.index(max(entries.shape))
    spots = []
    for shift in (0, 1):
        where = [jax.random.randint(jax.random.fold_in(rng, axis), (), 0, length) for axis, length in enumerate(entries.shape)]
        where[longest] = (where[longest] + shift) % entries.shape[longest]
        spots.append(tuple(where))
    return entries.at[spots[0]].set(least).at[spots[1]].set(top_value)


def setup_inputs(seed: int = 0) -> dict:
    key_of = jax.random.split(jax.random.key(seed), 5)
    return {
        "inputs": draw_inputs(jax.random.fold_in(key_of[4], 71), 0),
        "qkv_weight": draw_qkv_weight(jax.random.fold_in(key_of[4], 71), 0),
        "norm_gain": jnp.clip(1.0 + 0.15 * jax.random.normal(key_of[2], (SECTIONS, D), jnp.float32), 0.25, 1.75).astype(jnp.bfloat16),
        "preempted": plant((jax.random.randint(key_of[3], (SECTIONS,), 0, 4) < 1).astype(jnp.int32), jax.random.fold_in(key_of[3], 1), 0, 1),
    }


def attention_layer(hidden_in, weight, gain_row):
    float_acts = hidden_in.astype(jnp.float32)
    inverse_rms = lax.rsqrt(lax.optimization_barrier(jnp.mean(float_acts * float_acts, axis=-1, keepdims=True)) + 1e-05)
    normed = (float_acts * inverse_rms * gain_row).astype(jnp.bfloat16)
    flat_rows = normed.reshape(-1, D)
    head_shape = (hidden_in.shape[0], LEN, HEADS, HD)
    queries = jnp.dot(flat_rows, weight[0], preferred_element_type=jnp.float32).astype(jnp.bfloat16).reshape(head_shape)
    key_rows = jnp.dot(flat_rows, weight[1], preferred_element_type=jnp.float32).astype(jnp.bfloat16).reshape(head_shape)
    values = jnp.dot(flat_rows, weight[2], preferred_element_type=jnp.float32).astype(jnp.bfloat16).reshape(head_shape)
    scores = jnp.einsum('sqhd,skhd->shqk', queries.astype(jnp.float32), key_rows.astype(jnp.float32)) / jnp.sqrt(jnp.float32(HD))
    causal = jnp.arange(LEN)[:, None] >= jnp.arange(LEN)[None, :]
    scores = jnp.where(causal, scores, jnp.float32(-1e+30))
    probability = jax.nn.softmax(scores, axis=-1).astype(jnp.bfloat16)
    mixture = jnp.einsum('shqk,skhd->sqhd', probability.astype(jnp.float32), values.astype(jnp.float32))
    return (float_acts + mixture.reshape(hidden_in.shape)).astype(jnp.bfloat16)

def reference(inputs, qkv_weight, norm_gain, preempted):
    own_out = lax.map(lambda section_item: attention_layer(section_item[0], section_item[1], section_item[2]), (inputs, qkv_weight, norm_gain))
    before = jnp.concatenate([jnp.zeros_like(own_out[:1]), own_out[:-1]], axis=0)
    shadow = lax.map(lambda section_item: attention_layer(section_item[0], section_item[1], section_item[2]), (before, qkv_weight, norm_gain))
    return jnp.where((preempted == 1)[:, None, None, None], shadow, own_out)
```

```python
import functools
import math

import jax
import jax.numpy as jnp
from jax import lax
from jax.experimental import pallas as pl
from jax.experimental.pallas import tpu as pltpu
from jax.sharding import PartitionSpec as P

HD = 128
LAG = 3
MESH = pl.DeviceIdType.MESH


def kernel(
    sections,
    heads,
    a_hbm,
    w_hbm,
    gain_hbm,
    pre_ref,
    out_hbm,
    w,
    feats,
    psend,
    precv,
    a_own,
    x_prev,
    own,
    final,
    gain,
    squares,
    scale,
    note,
    heard,
    w_sem,
    in_sem,
    out_sem,
    q_send,
    q_recv,
    p_send,
    p_recv,
    s_send,
    s_recv,
    part_send,
    part_recv,
    hop_send,
    hop_recv,
    note_send,
    note_recv,
):
    s, d, t = lax.axis_index("section"), lax.axis_index("dp"), lax.axis_index("tensor")
    high, core = t // 2, t % 2
    rows, width = a_own.shape
    features = 4 * width

    partner = (s, 1 - d, t)
    other = (s, 1 - d, (1 - high) * 2 + core)
    sibling = (s, d, high * 2 + 1 - core)
    opposite = (s, d, (1 - high) * 2 + core)
    after = (lax.rem(s + 1, sections), d, t)
    before = (lax.rem(s + sections - 1, sections), d, t)

    straight = high == d
    mine = jnp.where(straight, 1, 2)
    to_other = jnp.where(straight, 2, 0)
    to_partner = jnp.where(straight, 1, 0)
    from_partner = jnp.where(straight, 0, 1)

    def columns(c, h):
        return pl.ds(pl.multiple_of(c * width + h * HD, HD), HD)

    def piece(layer, slot, c, h):
        return feats.at[layer, slot, :, columns(c, h)]

    def remote(src, dst, send, recv, device):
        return pltpu.make_async_remote_copy(
            src_ref=src, dst_ref=dst, send_sem=send, recv_sem=recv, device_id=device, device_id_type=MESH
        )

    def other_copy(layer, h):
        return remote(
            piece(layer, mine, core, h), piece(layer, to_other, core, h),
            q_send.at[layer, h], q_recv.at[layer, h], other,
        )

    def other_arrival(layer, h):
        there = piece(layer, to_other, core, h)
        return remote(there, there, q_send.at[layer, h], q_recv.at[layer, h], other)

    def partner_copy(layer, h):
        return remote(
            piece(layer, 2, core, h), piece(layer, to_partner, core, h),
            p_send.at[layer, h], p_recv.at[layer, h], partner,
        )

    def partner_arrival(layer, h):
        there = piece(layer, from_partner, core, h)
        return remote(there, there, p_send.at[layer, h], p_recv.at[layer, h], partner)

    def sibling_copy(layer, slot, h):
        here = piece(layer, slot, core, h)
        return remote(here, here, s_send.at[layer, slot, h], s_recv.at[layer, slot, h], sibling)

    def sibling_arrival(layer, slot, h):
        there = piece(layer, slot, 1 - core, h)
        return remote(there, there, s_send.at[layer, slot, h], s_recv.at[layer, slot, h], sibling)

    def part_copy(layer, g):
        return remote(
            psend.at[layer, g], precv.at[layer, g], part_send.at[layer, g], part_recv.at[layer, g], partner
        )

    def hop_copy(h):
        here = pl.ds(pl.multiple_of(h * HD, HD), HD)
        return remote(own.at[:, here], x_prev.at[:, here], hop_send.at[h], hop_recv.at[h], after)

    def note_copy(layer, i):
        return remote(
            note.at[layer, i], heard.at[layer, i], note_send.at[layer, i], note_recv.at[layer, i],
            (sibling, opposite)[i],
        )

    def w_copy(g, j):
        return pltpu.make_async_copy(
            w_hbm.at[j, :, pl.ds(pl.multiple_of(g * HD, HD), HD)],
            w.at[g, :, pl.ds(j * HD, HD)],
            w_sem.at[g, j],
        )

    def out_copy(h):
        here = pl.ds(pl.multiple_of(h * HD, HD), HD)
        return pltpu.make_async_copy(final.at[:, here], out_hbm.at[:, here], out_sem.at[h])

    a_copy = pltpu.make_async_copy(a_hbm, a_own, in_sem.at[0])
    gain_copy = pltpu.make_async_copy(gain_hbm, gain, in_sem.at[1])
    a_copy.start()
    gain_copy.start()

    @pl.loop(0, heads)
    def _(g):
        for j in range(3):
            w_copy(g, j).start()

    barrier = pltpu.get_barrier_semaphore()
    for device in (partner, other, sibling, opposite, before):
        pl.semaphore_signal(barrier, inc=1, device_id=device, device_id_type=MESH)
    pl.semaphore_wait(barrier, 5)

    a_copy.wait()
    gain_copy.wait()

    def layer_input(layer, h):
        here = pl.ds(pl.multiple_of(h * HD, HD), HD)
        if layer == 0:
            return a_own[:, here].astype(jnp.float32)
        return jnp.where(s == 0, 0.0, x_prev[:, here].astype(jnp.float32))

    def send_piece(layer, h):
        if layer == 1:
            hop_copy(h).wait_recv()
        x = layer_input(layer, h)
        squares[layer] += x * x
        row = gain[0:1, pl.ds(pl.multiple_of(t * width + h * HD, HD), HD)].astype(jnp.float32)
        feats[layer, mine, :, columns(core, h)] = (x * row).astype(jnp.bfloat16)
        other_copy(layer, h).start()

        @pl.when(straight)
        def _():
            sibling_copy(layer, 1, h).start()

        @pl.when(jnp.logical_not(straight))
        def _():
            partner_copy(layer, h).start()

    def pass_on(layer, h):
        other_arrival(layer, h).wait_recv()

        @pl.when(straight)
        def _():
            partner_copy(layer, h).start()
            partner_arrival(layer, h).wait_recv()

        sibling_copy(layer, 0, h).start()

    def late_pass_on(layer, h):
        partner_arrival(layer, h).wait_recv()
        sibling_copy(layer, 1, h).start()

    def tell_squares(layer):
        sums = jnp.sum(squares[layer], axis=1, keepdims=True)
        note[layer, 0] = jnp.broadcast_to(sums, (rows, HD)).T[0:8, :]
        note_copy(layer, 0).start()

    def tell_pair(layer):
        note_copy(layer, 0).wait_recv()
        note[layer, 1] = note[layer, 0] + heard[layer, 0]
        note_copy(layer, 1).start()

    def take_squares(layer):
        note_copy(layer, 1).wait_recv()
        total = note[layer, 1] + heard[layer, 1]
        inverse = lax.rsqrt(total * (1.0 / features) + 1e-05)
        scale[layer] = jnp.broadcast_to(inverse[0:1, :], (HD, rows)).T

    def send_parts(layer):
        @pl.loop(0, heads)
        def _(h):
            sibling_arrival(layer, 0, h).wait_recv()

        @pl.loop(0, heads)
        def _(g):
            if layer == 0:
                for j in range(3):
                    w_copy(g, j).wait()
            part = jnp.dot(feats[layer, 0], w[g], preferred_element_type=jnp.float32)
            psend[layer, g] = part.astype(jnp.bfloat16)
            part_copy(layer, g).start()

    def late_pieces(layer):
        @pl.when(jnp.logical_not(straight))
        def _():
            @pl.loop(0, heads)
            def _(h):
                late_pass_on(layer, h)

        @pl.loop(0, heads)
        def _(h):
            sibling_arrival(layer, 1, h).wait_recv()

    def attend(layer, g):
        part = jnp.dot(feats[layer, 1], w[g], preferred_element_type=jnp.float32)
        part_copy(layer, g).wait_recv()
        part = part + precv[layer, g].astype(jnp.float32)
        inverse = scale[layer]
        query = (part[:, 0:HD] * inverse).astype(jnp.bfloat16)
        key = (part[:, HD : 2 * HD] * inverse).astype(jnp.bfloat16)
        value = (part[:, 2 * HD :] * inverse).astype(jnp.bfloat16)
        scores = lax.dot_general(
            query, key, (((1,), (1,)), ((), ())), preferred_element_type=jnp.float32
        ) * (1.0 / math.sqrt(HD))
        causal = lax.broadcasted_iota(jnp.int32, (rows, rows), 0) >= lax.broadcasted_iota(
            jnp.int32, (rows, rows), 1
        )
        scores = jnp.where(causal, scores, jnp.float32(-1e30))
        powers = jnp.exp(scores - jnp.max(scores, axis=1, keepdims=True))
        chance = (powers * (1.0 / jnp.sum(powers, axis=1, keepdims=True))).astype(jnp.bfloat16)
        mixture = jnp.dot(chance, value, preferred_element_type=jnp.float32)
        return (layer_input(layer, g) + mixture).astype(jnp.bfloat16)

    squares[...] = jnp.zeros_like(squares)

    @pl.loop(0, heads)
    def _(h):
        send_piece(0, h)

    tell_squares(0)

    @pl.loop(0, heads)
    def _(h):
        pass_on(0, h)

    tell_pair(0)
    send_parts(0)
    late_pieces(0)
    take_squares(0)

    @pl.loop(0, heads)
    def _(g):
        here = pl.ds(pl.multiple_of(g * HD, HD), HD)
        own[:, here] = attend(0, g)
        hop_copy(g).start()

        @pl.when(g >= LAG)
        def _():
            send_piece(1, g - LAG)

    @pl.loop(heads - LAG, heads)
    def _(h):
        pass_on(1, h - (heads - LAG))
        send_piece(1, h)

    tell_squares(1)

    @pl.loop(LAG, heads)
    def _(h):
        pass_on(1, h)

    tell_pair(1)
    send_parts(1)
    late_pieces(1)
    take_squares(1)
    take = pre_ref[0] == 1

    @pl.loop(0, heads)
    def _(g):
        here = pl.ds(pl.multiple_of(g * HD, HD), HD)
        shadow = attend(1, g)
        final[:, here] = jnp.where(take, shadow, own[:, here])
        out_copy(g).start()

    @pl.loop(0, heads)
    def _(h):
        for layer in range(2):
            other_copy(layer, h).wait_send()
            partner_copy(layer, h).wait_send()
            sibling_copy(layer, 0, h).wait_send()
            sibling_copy(layer, 1, h).wait_send()
            part_copy(layer, h).wait_send()
        hop_copy(h).wait_send()
        out_copy(h).wait()

    for layer in range(2):
        for i in range(2):
            note_copy(layer, i).wait_send()


def local(sections, inputs, qkv_weight, norm_gain, preempted):
    rows, width = inputs.shape[2:]
    heads = width // HD
    depth = qkv_weight.shape[2]
    bf16, f32 = jnp.bfloat16, jnp.float32
    dma = pltpu.SemaphoreType.DMA
    any_space = pl.BlockSpec(memory_space=pl.ANY)
    result = pl.pallas_call(
        functools.partial(kernel, sections, heads),
        out_shape=jax.ShapeDtypeStruct((rows, width), bf16),
        in_specs=[any_space, any_space, any_space, pl.BlockSpec(memory_space=pltpu.SMEM)],
        out_specs=any_space,
        scratch_shapes=[
            pltpu.VMEM((heads, depth, 3 * HD), bf16),
            pltpu.VMEM((2, 3, rows, depth), bf16),
            pltpu.VMEM((2, heads, rows, 3 * HD), bf16),
            pltpu.VMEM((2, heads, rows, 3 * HD), bf16),
            pltpu.VMEM((rows, width), bf16),
            pltpu.VMEM((rows, width), bf16),
            pltpu.VMEM((rows, width), bf16),
            pltpu.VMEM((rows, width), bf16),
            pltpu.VMEM((1, 4 * width), bf16),
            pltpu.VMEM((2, rows, HD), f32),
            pltpu.VMEM((2, rows, HD), f32),
            pltpu.VMEM((2, 2, 8, rows), f32),
            pltpu.VMEM((2, 2, 8, rows), f32),
            dma((heads, 3)),
            dma((2,)),
            dma((heads,)),
            dma((2, heads)),
            dma((2, heads)),
            dma((2, heads)),
            dma((2, heads)),
            dma((2, 2, heads)),
            dma((2, 2, heads)),
            dma((2, heads)),
            dma((2, heads)),
            dma((heads,)),
            dma((heads,)),
            dma((2, 2)),
            dma((2, 2)),
        ],
        compiler_params=pltpu.CompilerParams(
            collective_id=0, has_side_effects=True, vmem_limit_bytes=48 * 2**20
        ),
        cost_estimate=pl.CostEstimate(
            flops=8 * rows * depth * 3 * width, bytes_accessed=qkv_weight.size * 2, transcendentals=0
        ),
        name="relay",
    )(inputs[0, 0], qkv_weight[0], norm_gain, preempted)
    return result[None, None]


def solution(mesh):
    placed = (
        P("section", "dp", None, "tensor"),
        P("section", None, "dp", "tensor"),
        P("section", None),
        P("section"),
    )
    return jax.shard_map(
        functools.partial(local, mesh.shape["section"]),
        mesh=mesh,
        in_specs=placed,
        out_specs=P("section", "dp", None, "tensor"),
        check_vma=False,
    )
```

```python
import functools
import math

import jax
import jax.numpy as jnp
from jax import lax
from jax.experimental import pallas as pl
from jax.experimental.pallas import tpu as pltpu
from jax.sharding import PartitionSpec as P

HD = 128
BLOCKS = 2
PIECES = 2
AHEAD = 4
SEND_AT = 0
MESH = pl.DeviceIdType.MESH


def kernel(
    sections,
    heads,
    a_hbm,
    w_hbm,
    gain_hbm,
    pre_ref,
    out_ref,
    w,
    feats,
    psend,
    precv,
    a_own,
    x_prev,
    own,
    gain,
    keys,
    values,
    squares,
    scale,
    note,
    heard,
    w_sem,
    in_sem,
    q_send,
    q_recv,
    p_send,
    p_recv,
    s_send,
    s_recv,
    part_send,
    part_recv,
    hop_send,
    hop_recv,
    note_send,
    note_recv,
):
    s, d, t = lax.axis_index("section"), lax.axis_index("dp"), lax.axis_index("tensor")
    high, core = t // 2, t % 2
    width = a_own.shape[1]
    rows = a_own.shape[0] // BLOCKS
    features = 4 * width
    stages = 2 * BLOCKS

    partner = (s, 1 - d, t)
    other = (s, 1 - d, (1 - high) * 2 + core)
    sibling = (s, d, high * 2 + 1 - core)
    opposite = (s, d, (1 - high) * 2 + core)
    after = (lax.rem(s + 1, sections), d, t)
    before = (lax.rem(s + sections - 1, sections), d, t)

    straight = high == d
    crossed = jnp.logical_not(straight)
    mine = jnp.where(straight, 1, 3)
    to_partner = jnp.where(straight, 2, 0)
    from_partner = jnp.where(straight, 0, 2)

    def head_columns(h):
        return pl.ds(pl.multiple_of(h * HD, HD), HD)

    def tokens(block):
        return pl.ds(block * rows, rows)

    def piece_rows(r):
        return pl.ds(pl.multiple_of(r * (rows // PIECES), rows // PIECES), rows // PIECES)

    def piece(stage, slot, c, r):
        return feats.at[stage, slot, c, piece_rows(r)]

    def remote(src, dst, send, recv, device):
        return pltpu.make_async_remote_copy(
            src_ref=src, dst_ref=dst, send_sem=send, recv_sem=recv, device_id=device, device_id_type=MESH
        )

    def partner_copy(stage, r):
        return remote(
            piece(stage, mine, core, r), piece(stage, to_partner, core, r),
            p_send.at[stage, r], p_recv.at[stage, r], partner,
        )

    def partner_arrival(stage, r):
        there = piece(stage, from_partner, core, r)
        return remote(there, there, p_send.at[stage, r], p_recv.at[stage, r], partner)

    def other_copy(stage, slot, r):
        return remote(
            piece(stage, 3 - slot, core, r), piece(stage, slot, core, r),
            q_send.at[stage, slot, r], q_recv.at[stage, slot, r], other,
        )

    def other_arrival(stage, slot, r):
        there = piece(stage, slot, core, r)
        return remote(there, there, q_send.at[stage, slot, r], q_recv.at[stage, slot, r], other)

    def sibling_copy(stage, slot, h):
        here = piece(stage, slot, core, h)
        return remote(here, here, s_send.at[stage, slot, h], s_recv.at[stage, slot, h], sibling)

    def sibling_arrival(stage, slot, h):
        there = piece(stage, slot, 1 - core, h)
        return remote(there, there, s_send.at[stage, slot, h], s_recv.at[stage, slot, h], sibling)

    def part_copy(stage, g):
        return remote(
            psend.at[stage, g], precv.at[stage, g], part_send.at[stage, g], part_recv.at[stage, g], partner
        )

    def hop_copy(block, h):
        here = (tokens(block), head_columns(h))
        return remote(own.at[here], x_prev.at[here], hop_send.at[block, h], hop_recv.at[block, h], after)

    def note_copy(stage, i):
        return remote(
            note.at[stage, i], heard.at[stage, i], note_send.at[stage, i], note_recv.at[stage, i],
            (sibling, opposite)[i],
        )

    def w_copy(g, j):
        return pltpu.make_async_copy(
            w_hbm.at[j, :, head_columns(g)], w.at[g, :, pl.ds(j * HD, HD)], w_sem.at[g, j]
        )

    a_copy = pltpu.make_async_copy(a_hbm, a_own, in_sem.at[0])
    gain_copy = pltpu.make_async_copy(gain_hbm, gain, in_sem.at[1])
    a_copy.start()
    gain_copy.start()

    @pl.loop(0, heads)
    def _(g):
        for j in range(3):
            w_copy(g, j).start()

    barrier = pltpu.get_barrier_semaphore()
    for device in (partner, other, sibling, opposite, before):
        pl.semaphore_signal(barrier, inc=1, device_id=device, device_id_type=MESH)

    @pl.when(s == 0)
    def _():
        x_prev[...] = jnp.zeros_like(x_prev)

    a_copy.wait()
    gain_copy.wait()
    pl.semaphore_wait(barrier, 5)

    def layer_input(stage, where):
        if stage < BLOCKS:
            return a_own[where].astype(jnp.float32)
        return x_prev[where].astype(jnp.float32)

    def send_pieces(stage):
        block = stage % BLOCKS
        if stage >= BLOCKS:

            @pl.when(s > 0)
            def _():
                @pl.loop(0, heads)
                def _(h):
                    hop_copy(block, h).wait_recv()

        row = gain[0:1, pl.ds(pl.multiple_of(t * width, HD), width)].astype(jnp.float32)

        @pl.loop(0, PIECES)
        def _(r):
            first = pl.multiple_of(block * rows + r * (rows // PIECES), rows // PIECES)
            x = layer_input(stage, (pl.ds(first, rows // PIECES), slice(None)))
            feats[stage, mine, core, piece_rows(r)] = (x * row).astype(jnp.bfloat16)
            partner_copy(stage, r).start()

            @pl.when(straight)
            def _():
                sibling_copy(stage, 1, r).start()

            @pl.when(crossed)
            def _():
                other_copy(stage, 0, r).start()

            x = x * x
            squares[piece_rows(r)] = sum(x[:, h * HD : (h + 1) * HD] for h in range(heads))

        sums = jnp.sum(squares[...], axis=1, keepdims=True)
        note[stage, 0] = jnp.broadcast_to(sums, (rows, HD)).T[0:8, :]
        note_copy(stage, 0).start()

    def pass_on(stage):
        @pl.when(straight)
        def _():
            @pl.loop(0, PIECES)
            def _(r):
                partner_arrival(stage, r).wait_recv()
                sibling_copy(stage, 0, r).start()

        @pl.when(crossed)
        def _():
            @pl.loop(0, PIECES)
            def _(r):
                other_arrival(stage, 0, r).wait_recv()
                sibling_copy(stage, 0, r).start()
                partner_arrival(stage, r).wait_recv()
                other_copy(stage, 1, r).start()

    def other_sequence(stage):
        note_copy(stage, 0).wait_recv()
        note[stage, 1] = note[stage, 0] + heard[stage, 0]
        note_copy(stage, 1).start()

        @pl.loop(0, PIECES)
        def _(r):
            sibling_arrival(stage, 0, r).wait_recv()

    def late_pieces(stage):
        @pl.when(crossed)
        def _():
            @pl.loop(0, PIECES)
            def _(r):
                other_arrival(stage, 1, r).wait_recv()
                sibling_copy(stage, 1, r).start()

        note_copy(stage, 1).wait_recv()
        total = note[stage, 1] + heard[stage, 1]
        inverse = lax.rsqrt(total * (1.0 / features) + 1e-05)
        scale[...] = jnp.broadcast_to(inverse[0:1, :], (HD, rows)).T

        @pl.loop(0, PIECES)
        def _(r):
            sibling_arrival(stage, 1, r).wait_recv()

    def project(stage, slot, g):
        return sum(
            jnp.dot(feats[stage, slot, c], w[g, c * width : (c + 1) * width], preferred_element_type=jnp.float32)
            for c in range(2)
        )

    def send_part(stage, g):
        part = project(stage, 0, g)
        psend[stage, g] = part.astype(jnp.bfloat16)
        part_copy(stage, g).start()

    def attend(stage, g):
        block = stage % BLOCKS
        part = project(stage, 1, g)
        part_copy(stage, g).wait_recv()
        part = part + precv[stage, g].astype(jnp.float32)
        inverse = scale[...]
        query = (part[:, 0:HD] * inverse).astype(jnp.bfloat16)
        keys[g, tokens(block)] = (part[:, HD : 2 * HD] * inverse).astype(jnp.bfloat16)
        values[g, tokens(block)] = (part[:, 2 * HD :] * inverse).astype(jnp.bfloat16)
        seen = (block + 1) * rows
        scores = lax.dot_general(
            query, keys[g, 0:seen], (((1,), (1,)), ((), ())), preferred_element_type=jnp.float32
        ) * (1.0 / math.sqrt(HD))
        causal = lax.broadcasted_iota(jnp.int32, (rows, seen), 0) + block * rows >= lax.broadcasted_iota(
            jnp.int32, (rows, seen), 1
        )
        scores = jnp.where(causal, scores, jnp.float32(-1e30))
        powers = jnp.exp(scores - jnp.max(scores, axis=1, keepdims=True))
        chance = (powers * (1.0 / jnp.sum(powers, axis=1, keepdims=True))).astype(jnp.bfloat16)
        mixture = jnp.dot(chance, values[g, 0:seen], preferred_element_type=jnp.float32)
        return (layer_input(stage, (tokens(block), head_columns(g))) + mixture).astype(jnp.bfloat16)

    send_pieces(0)
    send_pieces(1)
    pass_on(0)

    other_sequence(0)

    @pl.loop(0, heads)
    def _(g):
        for j in range(3):
            w_copy(g, j).wait()

        @pl.when(g < AHEAD)
        def _():
            send_part(0, g)

    pass_on(1)
    other_sequence(1)
    take = pre_ref[0] == 1

    for stage in range(stages):
        layer, block = stage // BLOCKS, stage % BLOCKS
        late_pieces(stage)
        feeds = 1 <= stage < stages - 1

        @pl.loop(0, heads)
        def _(g):
            if feeds:

                @pl.when(g == heads - AHEAD)
                def _():
                    pass_on(stage + 1)
                    other_sequence(stage + 1)

            here = (tokens(block), head_columns(g))
            result = attend(stage, g)
            if layer == 0:
                own[here] = result

                @pl.when(s < sections - 1)
                def _():
                    hop_copy(block, g).start()

            else:
                out_ref[here] = jnp.where(take, result, own[here])

            coming = g + AHEAD
            if stage < stages - 1:
                send_part(stage + coming // heads, lax.rem(coming, heads))
            else:

                @pl.when(coming < heads)
                def _():
                    send_part(stage, coming)

            if feeds:

                @pl.when(g == SEND_AT)
                def _():
                    send_pieces(stage + 1)

    for stage in range(stages):

        @pl.loop(0, PIECES)
        def _(r):
            partner_copy(stage, r).wait_send()

            @pl.when(crossed)
            def _():
                other_copy(stage, 0, r).wait_send()
                other_copy(stage, 1, r).wait_send()

            sibling_copy(stage, 0, r).wait_send()
            sibling_copy(stage, 1, r).wait_send()

        @pl.loop(0, heads)
        def _(h):
            part_copy(stage, h).wait_send()
            if stage < BLOCKS:

                @pl.when(s < sections - 1)
                def _():
                    hop_copy(stage, h).wait_send()

        for i in range(2):
            note_copy(stage, i).wait_send()


def local(sections, inputs, qkv_weight, norm_gain, preempted):
    rows, width = inputs.shape[2:]
    heads = width // HD
    depth = qkv_weight.shape[2]
    stages, short = 2 * BLOCKS, rows // BLOCKS
    bf16, f32 = jnp.bfloat16, jnp.float32
    dma = pltpu.SemaphoreType.DMA
    hbm = pl.BlockSpec(memory_space=pltpu.HBM)
    result = pl.pallas_call(
        functools.partial(kernel, sections, heads),
        out_shape=jax.ShapeDtypeStruct((rows, width), bf16),
        in_specs=[hbm, hbm, hbm, pl.BlockSpec(memory_space=pltpu.SMEM)],
        out_specs=pl.BlockSpec(memory_space=pltpu.VMEM),
        scratch_shapes=[
            pltpu.VMEM((heads, depth, 3 * HD), bf16),
            pltpu.VMEM((stages, 4, 2, short, width), bf16),
            pltpu.VMEM((stages, heads, short, 3 * HD), bf16),
            pltpu.VMEM((stages, heads, short, 3 * HD), bf16),
            pltpu.VMEM((rows, width), bf16),
            pltpu.VMEM((rows, width), bf16),
            pltpu.VMEM((rows, width), bf16),
            pltpu.VMEM((1, 4 * width), bf16),
            pltpu.VMEM((heads, rows, HD), bf16),
            pltpu.VMEM((heads, rows, HD), bf16),
            pltpu.VMEM((short, HD), f32),
            pltpu.VMEM((short, HD), f32),
            pltpu.VMEM((stages, 2, 8, short), f32),
            pltpu.VMEM((stages, 2, 8, short), f32),
            dma((heads, 3)),
            dma((2,)),
            dma((stages, 2, PIECES)),
            dma((stages, 2, PIECES)),
            dma((stages, PIECES)),
            dma((stages, PIECES)),
            dma((stages, 2, PIECES)),
            dma((stages, 2, PIECES)),
            dma((stages, heads)),
            dma((stages, heads)),
            dma((BLOCKS, heads)),
            dma((BLOCKS, heads)),
            dma((stages, 2)),
            dma((stages, 2)),
        ],
        compiler_params=pltpu.CompilerParams(
            collective_id=0, has_side_effects=True, vmem_limit_bytes=55900000
        ),
        cost_estimate=pl.CostEstimate(
            flops=8 * rows * depth * 3 * width, bytes_accessed=qkv_weight.size * 2, transcendentals=0
        ),
        name="relay",
    )(inputs[0, 0], qkv_weight[0], norm_gain, preempted)
    return result[None, None]


def solution(mesh):
    placed = (
        P("section", "dp", None, "tensor"),
        P("section", None, "dp", "tensor"),
        P("section", None),
        P("section"),
    )
    return jax.shard_map(
        functools.partial(local, mesh.shape["section"]),
        mesh=mesh,
        in_specs=placed,
        out_specs=P("section", "dp", None, "tensor"),
        check_vma=False,
    )
```

```python
import functools
import math

import jax
import jax.numpy as jnp
from jax import lax
from jax.experimental import pallas as pl
from jax.experimental.pallas import tpu as pltpu
from jax.sharding import PartitionSpec as P

HD = 128
BLOCKS = 2
PIECES = 2
AHEAD = 4
SEND_AT = 0
DRAIN_AT = 5
COLUMN = 8
MESH = pl.DeviceIdType.MESH


def kernel(
    sections,
    heads,
    a_hbm,
    w_hbm,
    gain_hbm,
    pre_ref,
    out_ref,
    w,
    feats,
    psend,
    precv,
    a_own,
    x_prev,
    own,
    gain,
    keys,
    values,
    squares,
    scale,
    note,
    heard,
    w_sem,
    in_sem,
    q_send,
    q_recv,
    p_send,
    p_recv,
    s_send,
    s_recv,
    part_send,
    part_recv,
    hop_send,
    hop_recv,
    note_send,
    note_recv,
    ready,
):
    s, d, t = lax.axis_index("section"), lax.axis_index("dp"), lax.axis_index("tensor")
    high, core = t // 2, t % 2
    width = a_own.shape[1]
    rows = a_own.shape[0] // BLOCKS
    features = 4 * width
    stages = 2 * BLOCKS

    partner = (s, 1 - d, t)
    other = (s, 1 - d, (1 - high) * 2 + core)
    sibling = (s, d, high * 2 + 1 - core)
    opposite = (s, d, (1 - high) * 2 + core)
    after = (lax.rem(s + 1, sections), d, t)
    before = (lax.rem(s + sections - 1, sections), d, t)

    straight = high == d
    crossed = jnp.logical_not(straight)
    mine = jnp.where(straight, 1, 3)
    to_partner = jnp.where(straight, 2, 0)
    from_partner = jnp.where(straight, 0, 2)

    def head_columns(h):
        return pl.ds(pl.multiple_of(h * HD, HD), HD)

    def tokens(block):
        return pl.ds(block * rows, rows)

    def piece_rows(r):
        return pl.ds(pl.multiple_of(r * (rows // PIECES), rows // PIECES), rows // PIECES)

    def piece(stage, slot, c, r):
        return feats.at[stage, slot, c, piece_rows(r)]

    def remote(src, dst, send, recv, device):
        return pltpu.make_async_remote_copy(
            src_ref=src, dst_ref=dst, send_sem=send, recv_sem=recv, device_id=device, device_id_type=MESH
        )

    def partner_copy(stage, r):
        return remote(
            piece(stage, mine, core, r), piece(stage, to_partner, core, r),
            p_send.at[stage, r], p_recv.at[stage, r], partner,
        )

    def partner_arrival(stage, r):
        there = piece(stage, from_partner, core, r)
        return remote(there, there, p_send.at[stage, r], p_recv.at[stage, r], partner)

    def other_copy(stage, slot, r):
        return remote(
            piece(stage, 3 - slot, core, r), piece(stage, slot, core, r),
            q_send.at[stage, slot, r], q_recv.at[stage, slot, r], other,
        )

    def other_arrival(stage, slot, r):
        there = piece(stage, slot, core, r)
        return remote(there, there, q_send.at[stage, slot, r], q_recv.at[stage, slot, r], other)

    def sibling_copy(stage, slot, h):
        here = piece(stage, slot, core, h)
        return remote(here, here, s_send.at[stage, slot, h], s_recv.at[stage, slot, h], sibling)

    def sibling_arrival(stage, slot, h):
        there = piece(stage, slot, 1 - core, h)
        return remote(there, there, s_send.at[stage, slot, h], s_recv.at[stage, slot, h], sibling)

    def part_copy(stage, g, i):
        here = (stage, g, slice(None), (pl.ds(0, 2 * HD), pl.ds(2 * HD, HD))[i])
        return remote(
            psend.at[here], precv.at[here], part_send.at[i, stage, g], part_recv.at[i, stage, g], partner
        )

    def hop_copy(block, h):
        here = (tokens(block), head_columns(h))
        return remote(own.at[here], x_prev.at[here], hop_send.at[block, h], hop_recv.at[block, h], after)

    def note_copy(stage, i):
        return remote(
            note.at[stage, i], heard.at[stage, i], note_send.at[stage, i], note_recv.at[stage, i],
            (sibling, opposite)[i],
        )

    def w_copy(g, j):
        return pltpu.make_async_copy(
            w_hbm.at[j, :, head_columns(g)], w.at[g, :, pl.ds(j * HD, HD)], w_sem.at[g, j]
        )

    barrier = pltpu.get_barrier_semaphore()
    for device in (partner, other, sibling, opposite):
        pl.semaphore_signal(barrier, inc=1, device_id=device, device_id_type=MESH)

    first, last = s % COLUMN == 0, s % COLUMN == COLUMN - 1

    @pl.when(first & (s > 0))
    def _():
        pl.semaphore_signal(barrier, inc=1, device_id=before, device_id_type=MESH)

    @pl.when(jnp.logical_not(last))
    def _():
        pl.semaphore_signal(barrier, inc=1, device_id=after, device_id_type=MESH)

    a_copy = pltpu.make_async_copy(a_hbm, a_own, in_sem.at[0])
    gain_copy = pltpu.make_async_copy(gain_hbm, gain, in_sem.at[1])
    a_copy.start()
    gain_copy.start()

    @pl.when(s == 0)
    def _():
        x_prev[...] = jnp.zeros_like(x_prev)

    a_copy.wait()
    gain_copy.wait()
    pl.semaphore_wait(
        barrier, 4 + jnp.where(first, 0, 1) + jnp.where(last & (s < sections - 1), 1, 0)
    )

    @pl.when(jnp.logical_not(first))
    def _():
        pl.semaphore_signal(ready, inc=1, device_id=before, device_id_type=MESH)

    def layer_input(stage, where):
        if stage < BLOCKS:
            return a_own[where].astype(jnp.float32)
        return x_prev[where].astype(jnp.float32)

    def traveling(stage):
        return pl.when(s > 0) if stage >= BLOCKS else (lambda step: step())

    def send_pieces(stage):
        block = stage % BLOCKS
        if stage >= BLOCKS:

            @pl.when(s == 0)
            def _():
                squares[...] = jnp.zeros_like(squares)
                for slot in range(2):
                    feats[stage, slot] = jnp.zeros(feats.shape[2:], feats.dtype)

        @traveling(stage)
        def _():
            if stage >= BLOCKS:

                @pl.loop(0, heads)
                def _(h):
                    hop_copy(block, h).wait_recv()

            row = gain[0:1, pl.ds(pl.multiple_of(t * width, HD), width)].astype(jnp.float32)

            @pl.loop(0, PIECES)
            def _(r):
                first = pl.multiple_of(block * rows + r * (rows // PIECES), rows // PIECES)
                x = layer_input(stage, (pl.ds(first, rows // PIECES), slice(None)))
                feats[stage, mine, core, piece_rows(r)] = (x * row).astype(jnp.bfloat16)
                partner_copy(stage, r).start()

                @pl.when(straight)
                def _():
                    sibling_copy(stage, 1, r).start()

                @pl.when(crossed)
                def _():
                    other_copy(stage, 0, r).start()

                x = x * x
                squares[piece_rows(r)] = sum(x[:, h * HD : (h + 1) * HD] for h in range(heads))

        sums = jnp.sum(squares[...], axis=1, keepdims=True)
        note[stage, 0] = jnp.broadcast_to(sums, (rows, HD)).T[0:8, :]
        note_copy(stage, 0).start()

    def pass_on(stage):
        @traveling(stage)
        def _():
            @pl.when(straight)
            def _():
                @pl.loop(0, PIECES)
                def _(r):
                    partner_arrival(stage, r).wait_recv()
                    sibling_copy(stage, 0, r).start()

            @pl.when(crossed)
            def _():
                @pl.loop(0, PIECES)
                def _(r):
                    other_arrival(stage, 0, r).wait_recv()
                    sibling_copy(stage, 0, r).start()
                    partner_arrival(stage, r).wait_recv()
                    other_copy(stage, 1, r).start()

    def other_sequence(stage):
        note_copy(stage, 0).wait_recv()
        note[stage, 1] = note[stage, 0] + heard[stage, 0]
        note_copy(stage, 1).start()

        @traveling(stage)
        def _():
            @pl.loop(0, PIECES)
            def _(r):
                sibling_arrival(stage, 0, r).wait_recv()

    def late_pieces(stage):
        @traveling(stage)
        def _():
            @pl.when(crossed)
            def _():
                @pl.loop(0, PIECES)
                def _(r):
                    other_arrival(stage, 1, r).wait_recv()
                    sibling_copy(stage, 1, r).start()

        note_copy(stage, 1).wait_recv()
        total = note[stage, 1] + heard[stage, 1]
        inverse = lax.rsqrt(total * (1.0 / features) + 1e-05)
        scale[...] = jnp.broadcast_to(inverse[0:1, :], (HD, rows)).T

        @traveling(stage)
        def _():
            @pl.loop(0, PIECES)
            def _(r):
                sibling_arrival(stage, 1, r).wait_recv()

    def project(stage, slot, g):
        return sum(
            jnp.dot(feats[stage, slot, c], w[g, c * width : (c + 1) * width], preferred_element_type=jnp.float32)
            for c in range(2)
        )

    def send_part(stage, g):
        part = project(stage, 0, g)
        psend[stage, g] = part.astype(jnp.bfloat16)
        for i in range(2):
            part_copy(stage, g, i).start()

    def attend(stage, g):
        block = stage % BLOCKS
        part = project(stage, 1, g)
        part_copy(stage, g, 0).wait_recv()
        inverse = scale[...]
        query = (part[:, 0:HD] + precv[stage, g, :, 0:HD].astype(jnp.float32)) * inverse
        key = (part[:, HD : 2 * HD] + precv[stage, g, :, HD : 2 * HD].astype(jnp.float32)) * inverse
        query = query.astype(jnp.bfloat16)
        keys[g, tokens(block)] = key.astype(jnp.bfloat16)
        seen = (block + 1) * rows
        scores = lax.dot_general(
            query, keys[g, 0:seen], (((1,), (1,)), ((), ())), preferred_element_type=jnp.float32
        ) * (1.0 / math.sqrt(HD))
        causal = lax.broadcasted_iota(jnp.int32, (rows, seen), 0) + block * rows >= lax.broadcasted_iota(
            jnp.int32, (rows, seen), 1
        )
        scores = jnp.where(causal, scores, jnp.float32(-1e30))
        powers = jnp.exp(scores - jnp.max(scores, axis=1, keepdims=True))
        chance = (powers * (1.0 / jnp.sum(powers, axis=1, keepdims=True))).astype(jnp.bfloat16)
        part_copy(stage, g, 1).wait_recv()
        value = (part[:, 2 * HD :] + precv[stage, g, :, 2 * HD :].astype(jnp.float32)) * inverse
        values[g, tokens(block)] = value.astype(jnp.bfloat16)
        mixture = jnp.dot(chance, values[g, 0:seen], preferred_element_type=jnp.float32)
        return (layer_input(stage, (tokens(block), head_columns(g))) + mixture).astype(jnp.bfloat16)

    def sent(stage):
        @traveling(stage)
        def _():
            @pl.loop(0, PIECES)
            def _(r):
                partner_copy(stage, r).wait_send()

                @pl.when(crossed)
                def _():
                    other_copy(stage, 0, r).wait_send()
                    other_copy(stage, 1, r).wait_send()

                sibling_copy(stage, 0, r).wait_send()
                sibling_copy(stage, 1, r).wait_send()

        for i in range(2):
            note_copy(stage, i).wait_send()

    def hops_sent(block):
        @pl.when(s < sections - 1)
        def _():
            @pl.loop(0, heads)
            def _(h):
                hop_copy(block, h).wait_send()

    send_pieces(0)

    @pl.loop(0, heads)
    def _(g):
        for j in range(3):
            w_copy(g, j).start()

    send_pieces(1)
    pass_on(0)

    other_sequence(0)

    @pl.loop(0, heads)
    def _(g):
        for j in range(3):
            w_copy(g, j).wait()

        @pl.when(g < AHEAD)
        def _():
            send_part(0, g)

    pass_on(1)
    other_sequence(1)

    @pl.when(jnp.logical_not(last))
    def _():
        pl.semaphore_wait(ready, 1)

    take = pre_ref[0] == 1

    for stage in range(stages):
        layer, block = stage // BLOCKS, stage % BLOCKS
        late_pieces(stage)
        feeds = 1 <= stage < stages - 1

        @pl.loop(0, heads)
        def _(g):
            if feeds:

                @pl.when(g == heads - AHEAD)
                def _():
                    pass_on(stage + 1)
                    other_sequence(stage + 1)

            coming = g + AHEAD
            if stage < stages - 1:
                send_part(stage + coming // heads, lax.rem(coming, heads))
            else:

                @pl.when(coming < heads)
                def _():
                    send_part(stage, coming)

            @pl.when(g == DRAIN_AT)
            def _():
                sent(stage)
                if layer > 0:
                    hops_sent(block)

            here = (tokens(block), head_columns(g))
            result = attend(stage, g)
            if layer == 0:
                own[here] = result

                @pl.when(s < sections - 1)
                def _():
                    hop_copy(block, g).start()

            else:
                out_ref[here] = jnp.where(take, result, own[here])

            for i in range(2):
                part_copy(stage, g, i).wait_send()

            if feeds:

                @pl.when(g == SEND_AT)
                def _():
                    send_pieces(stage + 1)


def local(sections, inputs, qkv_weight, norm_gain, preempted):
    rows, width = inputs.shape[2:]
    heads = width // HD
    depth = qkv_weight.shape[2]
    stages, short = 2 * BLOCKS, rows // BLOCKS
    bf16, f32 = jnp.bfloat16, jnp.float32
    dma = pltpu.SemaphoreType.DMA
    hbm = pl.BlockSpec(memory_space=pltpu.HBM)
    operands = (inputs[0, 0], qkv_weight[0], norm_gain)
    result = pl.pallas_call(
        functools.partial(kernel, sections, heads),
        out_shape=jax.ShapeDtypeStruct((rows, width), bf16),
        in_specs=[hbm, hbm, hbm, pl.BlockSpec(memory_space=pltpu.SMEM)],
        out_specs=pl.BlockSpec(memory_space=pltpu.VMEM),
        scratch_shapes=[
            pltpu.VMEM((heads, depth, 3 * HD), bf16),
            pltpu.VMEM((stages, 4, 2, short, width), bf16),
            pltpu.VMEM((stages, heads, short, 3 * HD), bf16),
            pltpu.VMEM((stages, heads, short, 3 * HD), bf16),
            pltpu.VMEM((rows, width), bf16),
            pltpu.VMEM((rows, width), bf16),
            pltpu.VMEM((rows, width), bf16),
            pltpu.VMEM((1, 4 * width), bf16),
            pltpu.VMEM((heads, rows, HD), bf16),
            pltpu.VMEM((heads, rows, HD), bf16),
            pltpu.VMEM((short, HD), f32),
            pltpu.VMEM((short, HD), f32),
            pltpu.VMEM((stages, 2, 8, short), f32),
            pltpu.VMEM((stages, 2, 8, short), f32),
            dma((heads, 3)),
            dma((2,)),
            dma((stages, 2, PIECES)),
            dma((stages, 2, PIECES)),
            dma((stages, PIECES)),
            dma((stages, PIECES)),
            dma((stages, 2, PIECES)),
            dma((stages, 2, PIECES)),
            dma((2, stages, heads)),
            dma((2, stages, heads)),
            dma((BLOCKS, heads)),
            dma((BLOCKS, heads)),
            dma((stages, 2)),
            dma((stages, 2)),
            pltpu.SemaphoreType.REGULAR,
        ],
        compiler_params=pltpu.CompilerParams(
            collective_id=0, has_side_effects=True, vmem_limit_bytes=48 * 2**20
        ),
        cost_estimate=pl.CostEstimate(
            flops=8 * rows * depth * 3 * width, bytes_accessed=qkv_weight.size * 2, transcendentals=0
        ),
        name="relay",
    )(*(pltpu.with_memory_space_constraint(x, pltpu.HBM) for x in operands), preempted)
    return result[None, None]


def solution(mesh):
    placed = (
        P("section", "dp", None, "tensor"),
        P("section", None, "dp", "tensor"),
        P("section", None),
        P("section"),
    )
    return jax.shard_map(
        functools.partial(local, mesh.shape["section"]),
        mesh=mesh,
        in_specs=placed,
        out_specs=P("section", "dp", None, "tensor"),
        check_vma=False,
    )
```

```python
import functools
import math

import jax
import jax.numpy as jnp
from jax import lax
from jax.experimental import pallas as pl
from jax.experimental.pallas import tpu as pltpu
from jax.sharding import PartitionSpec as P

HD = 128
BLOCKS = 2
PIECES = 1
AHEAD = 4
SEND_AT = 1
PASS_AT = 4
COLUMN = 8
MESH = pl.DeviceIdType.MESH


def kernel(
    sections,
    heads,
    a_hbm,
    w_hbm,
    gain_hbm,
    pre_ref,
    out_ref,
    w,
    feats,
    psend,
    precv,
    a_own,
    x_prev,
    own,
    gain,
    keys,
    values,
    squares,
    scale,
    note,
    heard,
    w_sem,
    in_sem,
    q_send,
    q_recv,
    p_send,
    p_recv,
    s_send,
    s_recv,
    part_send,
    part_recv,
    hop_send,
    hop_recv,
    note_send,
    note_recv,
    ready,
):
    s, d, t = lax.axis_index("section"), lax.axis_index("dp"), lax.axis_index("tensor")
    high, core = t // 2, t % 2
    width = a_own.shape[1]
    rows = a_own.shape[0] // BLOCKS
    features = 4 * width
    stages = 2 * BLOCKS

    partner = (s, 1 - d, t)
    other = (s, 1 - d, (1 - high) * 2 + core)
    sibling = (s, d, high * 2 + 1 - core)
    opposite = (s, d, (1 - high) * 2 + core)
    after = (lax.rem(s + 1, sections), d, t)
    before = (lax.rem(s + sections - 1, sections), d, t)

    straight = high == d
    crossed = jnp.logical_not(straight)
    mine = jnp.where(straight, 1, 3)
    to_partner = jnp.where(straight, 2, 0)
    from_partner = jnp.where(straight, 0, 2)

    def head_columns(h):
        return pl.ds(pl.multiple_of(h * HD, HD), HD)

    def tokens(block):
        return pl.ds(block * rows, rows)

    def piece_rows(r):
        return pl.ds(pl.multiple_of(r * (rows // PIECES), rows // PIECES), rows // PIECES)

    def piece(stage, slot, c, r):
        return feats.at[stage, slot, c, piece_rows(r)]

    def remote(src, dst, send, recv, device):
        return pltpu.make_async_remote_copy(
            src_ref=src, dst_ref=dst, send_sem=send, recv_sem=recv, device_id=device, device_id_type=MESH
        )

    def partner_copy(stage, r):
        return remote(
            piece(stage, mine, core, r), piece(stage, to_partner, core, r),
            p_send.at[stage, r], p_recv.at[stage, r], partner,
        )

    def partner_arrival(stage, r):
        there = piece(stage, from_partner, core, r)
        return remote(there, there, p_send.at[stage, r], p_recv.at[stage, r], partner)

    def other_copy(stage, slot, r):
        return remote(
            piece(stage, 3 - slot, core, r), piece(stage, slot, core, r),
            q_send.at[stage, slot, r], q_recv.at[stage, slot, r], other,
        )

    def other_arrival(stage, slot, r):
        there = piece(stage, slot, core, r)
        return remote(there, there, q_send.at[stage, slot, r], q_recv.at[stage, slot, r], other)

    def sibling_copy(stage, slot, h):
        here = piece(stage, slot, core, h)
        return remote(here, here, s_send.at[stage, slot, h], s_recv.at[stage, slot, h], sibling)

    def sibling_arrival(stage, slot, h):
        there = piece(stage, slot, 1 - core, h)
        return remote(there, there, s_send.at[stage, slot, h], s_recv.at[stage, slot, h], sibling)

    def part_copy(stage, g, i):
        here = (stage, g, slice(None), (pl.ds(0, 2 * HD), pl.ds(2 * HD, HD))[i])
        return remote(
            psend.at[here], precv.at[here], part_send.at[i, stage, g], part_recv.at[i, stage, g], partner
        )

    def hop_copy(block, h):
        here = (tokens(block), head_columns(h))
        return remote(own.at[here], x_prev.at[here], hop_send.at[block, h], hop_recv.at[block, h], after)

    def note_copy(stage, i):
        return remote(
            note.at[stage, i], heard.at[stage, i], note_send.at[stage, i], note_recv.at[stage, i],
            (sibling, opposite)[i],
        )

    def w_copy(g, j):
        return pltpu.make_async_copy(
            w_hbm.at[j, :, head_columns(g)], w.at[g, :, pl.ds(j * HD, HD)], w_sem.at[g, j]
        )

    def a_copy(block):
        return pltpu.make_async_copy(a_hbm.at[tokens(block)], a_own.at[tokens(block)], in_sem.at[block])

    gain_copy = pltpu.make_async_copy(gain_hbm, gain, in_sem.at[BLOCKS])
    a_copy(0).start()
    gain_copy.start()
    barrier = pltpu.get_barrier_semaphore()
    for device in (opposite, partner, sibling):
        pl.semaphore_signal(barrier, inc=1, device_id=device, device_id_type=MESH)

    @pl.when(crossed)
    def _():
        pl.semaphore_signal(barrier, inc=1, device_id=other, device_id_type=MESH)

    first, last = s % COLUMN == 0, s % COLUMN == COLUMN - 1

    @pl.when(first & (s > 0))
    def _():
        pl.semaphore_signal(barrier, inc=1, device_id=before, device_id_type=MESH)

    @pl.when(jnp.logical_not(last))
    def _():
        pl.semaphore_signal(barrier, inc=1, device_id=after, device_id_type=MESH)

    for block in range(1, BLOCKS):
        a_copy(block).start()

    @pl.when(s == 0)
    def _():
        x_prev[...] = jnp.zeros_like(x_prev)

    def layer_input(stage, where):
        if stage < BLOCKS:
            return a_own[where].astype(jnp.float32)
        return x_prev[where].astype(jnp.float32)

    def traveling(stage):
        return pl.when(s > 0) if stage >= BLOCKS else (lambda step: step())

    def make_pieces(stage):
        block = stage % BLOCKS
        if stage >= BLOCKS:

            @pl.when(s == 0)
            def _():
                squares[...] = jnp.zeros_like(squares)
                for slot in range(2):
                    feats[stage, slot] = jnp.zeros(feats.shape[2:], feats.dtype)

        @traveling(stage)
        def _():
            if stage >= BLOCKS:

                @pl.loop(0, heads)
                def _(h):
                    hop_copy(block, h).wait_recv()

            row = gain[0:1, pl.ds(pl.multiple_of(t * width, HD), width)].astype(jnp.float32)

            @pl.loop(0, PIECES)
            def _(r):
                first = pl.multiple_of(block * rows + r * (rows // PIECES), rows // PIECES)
                x = layer_input(stage, (pl.ds(first, rows // PIECES), slice(None)))
                feats[stage, mine, core, piece_rows(r)] = (x * row).astype(jnp.bfloat16)
                if stage >= BLOCKS:
                    send_piece(stage, r)
                x = x * x
                squares[piece_rows(r)] = sum(x[:, h * HD : (h + 1) * HD] for h in range(heads))

        sums = jnp.sum(squares[...], axis=1, keepdims=True)
        note[stage, 0] = jnp.broadcast_to(sums, (rows, HD)).T[0:8, :]
        if stage >= BLOCKS:
            note_copy(stage, 0).start()

    def send_piece(stage, r):
        partner_copy(stage, r).start()

        @pl.when(straight)
        def _():
            sibling_copy(stage, 1, r).start()

        @pl.when(crossed)
        def _():
            other_copy(stage, 0, r).start()

    def pass_on(stage):
        @traveling(stage)
        def _():
            @pl.when(straight)
            def _():
                @pl.loop(0, PIECES)
                def _(r):
                    partner_arrival(stage, r).wait_recv()
                    sibling_copy(stage, 0, r).start()

            @pl.when(crossed)
            def _():
                @pl.loop(0, PIECES)
                def _(r):
                    other_arrival(stage, 0, r).wait_recv()
                    sibling_copy(stage, 0, r).start()
                    partner_arrival(stage, r).wait_recv()
                    other_copy(stage, 1, r).start()

    def other_sequence(stage):
        note_copy(stage, 0).wait_recv()
        note[stage, 1] = note[stage, 0] + heard[stage, 0]
        note_copy(stage, 1).start()

        @traveling(stage)
        def _():
            @pl.loop(0, PIECES)
            def _(r):
                sibling_arrival(stage, 0, r).wait_recv()

    def late_pieces(stage):
        @traveling(stage)
        def _():
            @pl.when(crossed)
            def _():
                @pl.loop(0, PIECES)
                def _(r):
                    other_arrival(stage, 1, r).wait_recv()
                    sibling_copy(stage, 1, r).start()

        note_copy(stage, 1).wait_recv()
        total = note[stage, 1] + heard[stage, 1]
        inverse = lax.rsqrt(total * (1.0 / features) + 1e-05)
        scale[...] = jnp.broadcast_to(inverse[0:1, :], (HD, rows)).T

        @traveling(stage)
        def _():
            @pl.loop(0, PIECES)
            def _(r):
                sibling_arrival(stage, 1, r).wait_recv()

    def project(stage, slot, g):
        return sum(
            jnp.dot(feats[stage, slot, c], w[g, c * width : (c + 1) * width], preferred_element_type=jnp.float32)
            for c in range(2)
        )

    def send_part(stage, g):
        part = project(stage, 0, g)
        psend[stage, g] = part.astype(jnp.bfloat16)
        for i in range(2):
            part_copy(stage, g, i).start()

    def attend(stage, g):
        block = stage % BLOCKS
        part = project(stage, 1, g)
        part_copy(stage, g, 0).wait_recv()
        inverse = scale[...]
        query = (part[:, 0:HD] + precv[stage, g, :, 0:HD].astype(jnp.float32)) * inverse
        key = (part[:, HD : 2 * HD] + precv[stage, g, :, HD : 2 * HD].astype(jnp.float32)) * inverse
        query = query.astype(jnp.bfloat16)
        keys[g, tokens(block)] = key.astype(jnp.bfloat16)
        seen = (block + 1) * rows
        scores = lax.dot_general(
            query, keys[g, 0:seen], (((1,), (1,)), ((), ())), preferred_element_type=jnp.float32
        ) * (1.0 / math.sqrt(HD))
        causal = lax.broadcasted_iota(jnp.int32, (rows, seen), 0) + block * rows >= lax.broadcasted_iota(
            jnp.int32, (rows, seen), 1
        )
        scores = jnp.where(causal, scores, jnp.float32(-1e30))
        powers = jnp.exp(scores - jnp.max(scores, axis=1, keepdims=True))
        chance = (powers * (1.0 / jnp.sum(powers, axis=1, keepdims=True))).astype(jnp.bfloat16)
        part_copy(stage, g, 1).wait_recv()
        value = (part[:, 2 * HD :] + precv[stage, g, :, 2 * HD :].astype(jnp.float32)) * inverse
        values[g, tokens(block)] = value.astype(jnp.bfloat16)
        mixture = jnp.dot(chance, values[g, 0:seen], preferred_element_type=jnp.float32)
        return (layer_input(stage, (tokens(block), head_columns(g))) + mixture).astype(jnp.bfloat16)

    def sent(stage):
        @traveling(stage)
        def _():
            @pl.loop(0, PIECES)
            def _(r):
                partner_copy(stage, r).wait_send()

                @pl.when(crossed)
                def _():
                    other_copy(stage, 0, r).wait_send()
                    other_copy(stage, 1, r).wait_send()

                sibling_copy(stage, 0, r).wait_send()
                sibling_copy(stage, 1, r).wait_send()

        for i in range(2):
            note_copy(stage, i).wait_send()

    def hops_sent(block):
        @pl.when(s < sections - 1)
        def _():
            @pl.loop(0, heads)
            def _(h):
                hop_copy(block, h).wait_send()

    gain_copy.wait()
    for block in range(BLOCKS):
        a_copy(block).wait()
        make_pieces(block)

    pl.semaphore_wait(
        barrier, 3 + jnp.where(crossed, 1, 0) + jnp.where(first, 0, 1) + jnp.where(last & (s < sections - 1), 1, 0)
    )

    @pl.when(jnp.logical_not(first))
    def _():
        pl.semaphore_signal(ready, inc=1, device_id=before, device_id_type=MESH)

    for block in range(BLOCKS):

        @pl.loop(0, PIECES)
        def _(r):
            send_piece(block, r)

        note_copy(block, 0).start()

    @pl.loop(0, heads)
    def _(g):
        for j in range(3):
            w_copy(g, j).start()

    pass_on(0)

    other_sequence(0)

    @pl.loop(0, heads)
    def _(g):
        for j in range(3):
            w_copy(g, j).wait()

        @pl.when(g < AHEAD)
        def _():
            send_part(0, g)

    pass_on(1)
    other_sequence(1)

    @pl.when(jnp.logical_not(last))
    def _():
        pl.semaphore_wait(ready, 1)

    take = pre_ref[0] == 1

    for stage in range(stages):
        layer, block = stage // BLOCKS, stage % BLOCKS
        late_pieces(stage)
        feeds = 1 <= stage < stages - 1

        @pl.loop(0, heads)
        def _(g):
            if feeds:

                @pl.when(g == SEND_AT)
                def _():
                    make_pieces(stage + 1)

                @pl.when(g == PASS_AT)
                def _():
                    pass_on(stage + 1)
                    other_sequence(stage + 1)

            @pl.when(g == PASS_AT - 1)
            def _():
                sent(stage)
                if layer > 0:
                    hops_sent(block)

            coming = jnp.where(g < PASS_AT, g + AHEAD, g - PASS_AT + heads)
            ours = coming < heads

            @pl.when(ours if stage == stages - 1 else ours | (g >= PASS_AT))
            def _():
                send_part(stage + coming // heads, lax.rem(coming, heads))

            here = (tokens(block), head_columns(g))
            result = attend(stage, g)
            if layer == 0:
                own[here] = result

                @pl.when(s < sections - 1)
                def _():
                    hop_copy(block, g).start()

            else:
                out_ref[here] = jnp.where(take, result, own[here])

            for i in range(2):
                part_copy(stage, g, i).wait_send()

        if stage < stages - 1:
            for g in range(heads - PASS_AT, AHEAD):
                send_part(stage + 1, g)


def local(sections, inputs, qkv_weight, norm_gain, preempted):
    rows, width = inputs.shape[2:]
    heads = width // HD
    depth = qkv_weight.shape[2]
    stages, short = 2 * BLOCKS, rows // BLOCKS
    bf16, f32 = jnp.bfloat16, jnp.float32
    dma = pltpu.SemaphoreType.DMA
    hbm = pl.BlockSpec(memory_space=pltpu.HBM)
    operands = (inputs[0, 0], qkv_weight[0], norm_gain)
    result = pl.pallas_call(
        functools.partial(kernel, sections, heads),
        out_shape=jax.ShapeDtypeStruct((rows, width), bf16),
        in_specs=[hbm, hbm, hbm, pl.BlockSpec(memory_space=pltpu.SMEM)],
        out_specs=pl.BlockSpec(memory_space=pltpu.VMEM),
        scratch_shapes=[
            pltpu.VMEM((heads, depth, 3 * HD), bf16),
            pltpu.VMEM((stages, 4, 2, short, width), bf16),
            pltpu.VMEM((stages, heads, short, 3 * HD), bf16),
            pltpu.VMEM((stages, heads, short, 3 * HD), bf16),
            pltpu.VMEM((rows, width), bf16),
            pltpu.VMEM((rows, width), bf16),
            pltpu.VMEM((rows, width), bf16),
            pltpu.VMEM((1, 4 * width), bf16),
            pltpu.VMEM((heads, rows, HD), bf16),
            pltpu.VMEM((heads, rows, HD), bf16),
            pltpu.VMEM((short, HD), f32),
            pltpu.VMEM((short, HD), f32),
            pltpu.VMEM((stages, 2, 8, short), f32),
            pltpu.VMEM((stages, 2, 8, short), f32),
            dma((heads, 3)),
            dma((BLOCKS + 1,)),
            dma((stages, 2, PIECES)),
            dma((stages, 2, PIECES)),
            dma((stages, PIECES)),
            dma((stages, PIECES)),
            dma((stages, 2, PIECES)),
            dma((stages, 2, PIECES)),
            dma((2, stages, heads)),
            dma((2, stages, heads)),
            dma((BLOCKS, heads)),
            dma((BLOCKS, heads)),
            dma((stages, 2)),
            dma((stages, 2)),
            pltpu.SemaphoreType.REGULAR,
        ],
        compiler_params=pltpu.CompilerParams(
            collective_id=0, has_side_effects=True, vmem_limit_bytes=48 * 2**20
        ),
        cost_estimate=pl.CostEstimate(
            flops=8 * rows * depth * 3 * width, bytes_accessed=qkv_weight.size * 2, transcendentals=0
        ),
        name="relay",
    )(*(pltpu.with_memory_space_constraint(x, pltpu.HBM) for x in operands), preempted)
    return result[None, None]


def solution(mesh):
    placed = (
        P("section", "dp", None, "tensor"),
        P("section", None, "dp", "tensor"),
        P("section", None),
        P("section"),
    )
    return jax.shard_map(
        functools.partial(local, mesh.shape["section"]),
        mesh=mesh,
        in_specs=placed,
        out_specs=P("section", "dp", None, "tensor"),
        check_vma=False,
    )
```

```python
import functools
import math

import jax
import jax.numpy as jnp
from jax import lax
from jax.experimental import pallas as pl
from jax.experimental.pallas import tpu as pltpu
from jax.sharding import PartitionSpec as P

HD = 128
BLOCKS = 2
PIECES = 1
AHEAD = 5
SEND_AT = 0
PASS_AT = 4
COLUMN = 8
MESH = pl.DeviceIdType.MESH


def kernel(
    sections,
    heads,
    a_hbm,
    w_hbm,
    gain_hbm,
    pre_ref,
    out_ref,
    w,
    feats,
    psend,
    vsend,
    precv,
    vrecv,
    a_own,
    x_prev,
    own,
    gain,
    keys,
    values,
    squares,
    scale,
    note,
    heard,
    w_sem,
    in_sem,
    q_send,
    q_recv,
    p_send,
    p_recv,
    s_send,
    s_recv,
    part_send,
    part_recv,
    hop_send,
    hop_recv,
    note_send,
    note_recv,
    ready,
):
    s, d, t = lax.axis_index("section"), lax.axis_index("dp"), lax.axis_index("tensor")
    high, core = t // 2, t % 2
    width = a_own.shape[1]
    rows = a_own.shape[0] // BLOCKS
    features = 4 * width
    stages = 2 * BLOCKS

    partner = (s, 1 - d, t)
    other = (s, 1 - d, (1 - high) * 2 + core)
    sibling = (s, d, high * 2 + 1 - core)
    opposite = (s, d, (1 - high) * 2 + core)
    after = (lax.rem(s + 1, sections), d, t)
    before = (lax.rem(s + sections - 1, sections), d, t)

    straight = high == d
    crossed = jnp.logical_not(straight)
    mine = jnp.where(straight, 1, 3)
    to_partner = jnp.where(straight, 2, 0)
    from_partner = jnp.where(straight, 0, 2)

    def head_columns(h):
        return pl.ds(pl.multiple_of(h * HD, HD), HD)

    def tokens(block):
        return pl.ds(block * rows, rows)

    def piece_rows(r):
        return pl.ds(pl.multiple_of(r * (rows // PIECES), rows // PIECES), rows // PIECES)

    def piece(stage, slot, c, r):
        return feats.at[stage, slot, c, piece_rows(r)]

    def remote(src, dst, send, recv, device):
        return pltpu.make_async_remote_copy(
            src_ref=src, dst_ref=dst, send_sem=send, recv_sem=recv, device_id=device, device_id_type=MESH
        )

    def partner_copy(stage, r):
        return remote(
            piece(stage, mine, core, r), piece(stage, to_partner, core, r),
            p_send.at[stage, r], p_recv.at[stage, r], partner,
        )

    def partner_arrival(stage, r):
        there = piece(stage, from_partner, core, r)
        return remote(there, there, p_send.at[stage, r], p_recv.at[stage, r], partner)

    def other_copy(stage, slot, r):
        return remote(
            piece(stage, 3 - slot, core, r), piece(stage, slot, core, r),
            q_send.at[stage, slot, r], q_recv.at[stage, slot, r], other,
        )

    def other_arrival(stage, slot, r):
        there = piece(stage, slot, core, r)
        return remote(there, there, q_send.at[stage, slot, r], q_recv.at[stage, slot, r], other)

    def sibling_copy(stage, slot, h):
        here = piece(stage, slot, core, h)
        return remote(here, here, s_send.at[stage, slot, h], s_recv.at[stage, slot, h], sibling)

    def sibling_arrival(stage, slot, h):
        there = piece(stage, slot, 1 - core, h)
        return remote(there, there, s_send.at[stage, slot, h], s_recv.at[stage, slot, h], sibling)

    def part_copy(stage, g, i):
        return remote(
            (psend, vsend)[i].at[stage, g], (precv, vrecv)[i].at[stage, g],
            part_send.at[i, stage, g], part_recv.at[i, stage, g], partner,
        )

    def hop_copy(block, h):
        here = (tokens(block), head_columns(h))
        return remote(own.at[here], x_prev.at[here], hop_send.at[block, h], hop_recv.at[block, h], after)

    def note_copy(stage, i):
        return remote(
            note.at[stage, i], heard.at[stage, i], note_send.at[stage, i], note_recv.at[stage, i],
            (sibling, opposite)[i],
        )

    def w_copy(g, j):
        return pltpu.make_async_copy(
            w_hbm.at[j, :, head_columns(g)], w.at[g, :, pl.ds(j * HD, HD)], w_sem.at[g, j]
        )

    def a_copy(block):
        return pltpu.make_async_copy(a_hbm.at[tokens(block)], a_own.at[tokens(block)], in_sem.at[block])

    gain_copy = pltpu.make_async_copy(gain_hbm, gain, in_sem.at[BLOCKS])
    a_copy(0).start()
    gain_copy.start()
    barrier = pltpu.get_barrier_semaphore()
    for device in (opposite, partner, sibling):
        pl.semaphore_signal(barrier, inc=1, device_id=device, device_id_type=MESH)

    @pl.when(crossed)
    def _():
        pl.semaphore_signal(barrier, inc=1, device_id=other, device_id_type=MESH)

    first, last = s % COLUMN == 0, s % COLUMN == COLUMN - 1

    @pl.when(first & (s > 0))
    def _():
        pl.semaphore_signal(barrier, inc=1, device_id=before, device_id_type=MESH)

    @pl.when(jnp.logical_not(last))
    def _():
        pl.semaphore_signal(barrier, inc=1, device_id=after, device_id_type=MESH)

    for block in range(1, BLOCKS):
        a_copy(block).start()

    @pl.when(s == 0)
    def _():
        x_prev[...] = jnp.zeros_like(x_prev)

    def layer_input(stage, where):
        if stage < BLOCKS:
            return a_own[where].astype(jnp.float32)
        return x_prev[where].astype(jnp.float32)

    def traveling(stage):
        return pl.when(s > 0) if stage >= BLOCKS else (lambda step: step())

    def make_pieces(stage):
        block = stage % BLOCKS
        if stage >= BLOCKS:

            @pl.when(s == 0)
            def _():
                squares[...] = jnp.zeros_like(squares)
                for slot in range(2):
                    feats[stage, slot] = jnp.zeros(feats.shape[2:], feats.dtype)

        @traveling(stage)
        def _():
            if stage >= BLOCKS:

                @pl.loop(0, heads)
                def _(h):
                    hop_copy(block, h).wait_recv()

            row = gain[0:1, pl.ds(pl.multiple_of(t * width, HD), width)].astype(jnp.float32)

            @pl.loop(0, PIECES)
            def _(r):
                first = pl.multiple_of(block * rows + r * (rows // PIECES), rows // PIECES)
                x = layer_input(stage, (pl.ds(first, rows // PIECES), slice(None)))
                feats[stage, mine, core, piece_rows(r)] = (x * row).astype(jnp.bfloat16)
                if stage >= BLOCKS:
                    send_piece(stage, r)
                x = x * x
                squares[piece_rows(r)] = sum(x[:, h * HD : (h + 1) * HD] for h in range(heads))

        sums = jnp.sum(squares[...], axis=1, keepdims=True)
        note[stage, 0] = jnp.broadcast_to(sums, (rows, HD)).T[0:8, :]
        if stage >= BLOCKS:
            note_copy(stage, 0).start()

    def send_piece(stage, r):
        partner_copy(stage, r).start()

        @pl.when(straight)
        def _():
            sibling_copy(stage, 1, r).start()

        @pl.when(crossed)
        def _():
            other_copy(stage, 0, r).start()

    def pass_on(stage):
        @traveling(stage)
        def _():
            @pl.when(straight)
            def _():
                @pl.loop(0, PIECES)
                def _(r):
                    partner_arrival(stage, r).wait_recv()
                    sibling_copy(stage, 0, r).start()

            @pl.when(crossed)
            def _():
                @pl.loop(0, PIECES)
                def _(r):
                    other_arrival(stage, 0, r).wait_recv()
                    sibling_copy(stage, 0, r).start()
                    partner_arrival(stage, r).wait_recv()
                    other_copy(stage, 1, r).start()

    def other_sequence(stage):
        note_copy(stage, 0).wait_recv()
        note[stage, 1] = note[stage, 0] + heard[stage, 0]
        note_copy(stage, 1).start()

        @traveling(stage)
        def _():
            @pl.loop(0, PIECES)
            def _(r):
                sibling_arrival(stage, 0, r).wait_recv()

    def late_pieces(stage):
        @traveling(stage)
        def _():
            @pl.when(crossed)
            def _():
                @pl.loop(0, PIECES)
                def _(r):
                    other_arrival(stage, 1, r).wait_recv()
                    sibling_copy(stage, 1, r).start()

        note_copy(stage, 1).wait_recv()
        total = note[stage, 1] + heard[stage, 1]
        inverse = lax.rsqrt(total * (1.0 / features) + 1e-05)
        scale[...] = jnp.broadcast_to(inverse[0:1, :], (HD, rows)).T

        @traveling(stage)
        def _():
            @pl.loop(0, PIECES)
            def _(r):
                sibling_arrival(stage, 1, r).wait_recv()

    def project(stage, slot, g):
        return sum(
            jnp.dot(feats[stage, slot, c], w[g, c * width : (c + 1) * width], preferred_element_type=jnp.float32)
            for c in range(2)
        )

    def send_part(stage, g):
        part = project(stage, 0, g)
        psend[stage, g] = part[:, : 2 * HD].astype(jnp.bfloat16)
        vsend[stage, g] = part[:, 2 * HD :].astype(jnp.bfloat16)
        for i in range(2):
            part_copy(stage, g, i).start()

    def attend(stage, g):
        block = stage % BLOCKS
        part = project(stage, 1, g)
        part_copy(stage, g, 0).wait_recv()
        inverse = scale[...]
        query = (part[:, 0:HD] + precv[stage, g, :, 0:HD].astype(jnp.float32)) * inverse
        key = (part[:, HD : 2 * HD] + precv[stage, g, :, HD : 2 * HD].astype(jnp.float32)) * inverse
        query = query.astype(jnp.bfloat16)
        keys[g, tokens(block)] = key.astype(jnp.bfloat16)
        seen = (block + 1) * rows
        scores = lax.dot_general(
            query, keys[g, 0:seen], (((1,), (1,)), ((), ())), preferred_element_type=jnp.float32
        ) * (1.0 / math.sqrt(HD))
        causal = lax.broadcasted_iota(jnp.int32, (rows, seen), 0) + block * rows >= lax.broadcasted_iota(
            jnp.int32, (rows, seen), 1
        )
        scores = jnp.where(causal, scores, jnp.float32(-1e30))
        powers = jnp.exp(scores - jnp.max(scores, axis=1, keepdims=True))
        chance = (powers * (1.0 / jnp.sum(powers, axis=1, keepdims=True))).astype(jnp.bfloat16)
        part_copy(stage, g, 1).wait_recv()
        value = (part[:, 2 * HD :] + vrecv[stage, g].astype(jnp.float32)) * inverse
        values[g, tokens(block)] = value.astype(jnp.bfloat16)
        mixture = jnp.dot(chance, values[g, 0:seen], preferred_element_type=jnp.float32)
        return (layer_input(stage, (tokens(block), head_columns(g))) + mixture).astype(jnp.bfloat16)

    def sent(stage):
        @traveling(stage)
        def _():
            @pl.loop(0, PIECES)
            def _(r):
                partner_copy(stage, r).wait_send()

                @pl.when(crossed)
                def _():
                    other_copy(stage, 0, r).wait_send()
                    other_copy(stage, 1, r).wait_send()

                sibling_copy(stage, 0, r).wait_send()
                sibling_copy(stage, 1, r).wait_send()

        for i in range(2):
            note_copy(stage, i).wait_send()

    def hops_sent(block):
        @pl.when(s < sections - 1)
        def _():
            @pl.loop(0, heads)
            def _(h):
                hop_copy(block, h).wait_send()

    gain_copy.wait()
    a_copy(0).wait()
    make_pieces(0)

    pl.semaphore_wait(
        barrier, 3 + jnp.where(crossed, 1, 0) + jnp.where(first, 0, 1) + jnp.where(last & (s < sections - 1), 1, 0)
    )

    @pl.when(jnp.logical_not(first))
    def _():
        pl.semaphore_signal(ready, inc=1, device_id=before, device_id_type=MESH)

    for block in range(BLOCKS):
        if block > 0:
            a_copy(block).wait()
            make_pieces(block)

        @pl.loop(0, PIECES)
        def _(r):
            send_piece(block, r)

        note_copy(block, 0).start()

    @pl.loop(0, heads)
    def _(g):
        for j in range(3):
            w_copy(g, j).start()

    pass_on(0)

    other_sequence(0)

    @pl.loop(0, heads)
    def _(g):
        for j in range(3):
            w_copy(g, j).wait()

        @pl.when(g < AHEAD)
        def _():
            send_part(0, g)

    pass_on(1)
    other_sequence(1)

    @pl.when(jnp.logical_not(last))
    def _():
        pl.semaphore_wait(ready, 1)

    take = pre_ref[0] == 1

    for stage in range(stages):
        layer, block = stage // BLOCKS, stage % BLOCKS
        late_pieces(stage)
        feeds = 1 <= stage < stages - 1

        @pl.loop(0, heads)
        def _(g):
            if feeds:

                @pl.when(g == SEND_AT)
                def _():
                    make_pieces(stage + 1)

                @pl.when(g == PASS_AT)
                def _():
                    pass_on(stage + 1)
                    other_sequence(stage + 1)

            @pl.when(g == PASS_AT - 1)
            def _():
                sent(stage)
                if layer > 0:
                    hops_sent(block)

            coming = jnp.where(g < PASS_AT, g + AHEAD, g - PASS_AT + heads)
            ours = coming < heads

            @pl.when(ours if stage == stages - 1 else ours | (g >= PASS_AT))
            def _():
                send_part(stage + coming // heads, lax.rem(coming, heads))

            here = (tokens(block), head_columns(g))
            result = attend(stage, g)
            if layer == 0:
                own[here] = result

                @pl.when(s < sections - 1)
                def _():
                    hop_copy(block, g).start()

            else:
                out_ref[here] = jnp.where(take, result, own[here])

            for i in range(2):
                part_copy(stage, g, i).wait_send()

        if stage < stages - 1:
            for g in range(heads - PASS_AT, AHEAD):
                send_part(stage + 1, g)


def local(sections, inputs, qkv_weight, norm_gain, preempted):
    rows, width = inputs.shape[2:]
    heads = width // HD
    depth = qkv_weight.shape[2]
    stages, short = 2 * BLOCKS, rows // BLOCKS
    bf16, f32 = jnp.bfloat16, jnp.float32
    dma = pltpu.SemaphoreType.DMA
    hbm = pl.BlockSpec(memory_space=pltpu.HBM)
    operands = (inputs[0, 0], qkv_weight[0], norm_gain)
    result = pl.pallas_call(
        functools.partial(kernel, sections, heads),
        out_shape=jax.ShapeDtypeStruct((rows, width), bf16),
        in_specs=[hbm, hbm, hbm, pl.BlockSpec(memory_space=pltpu.SMEM)],
        out_specs=pl.BlockSpec(memory_space=pltpu.VMEM),
        scratch_shapes=[
            pltpu.VMEM((heads, depth, 3 * HD), bf16),
            pltpu.VMEM((stages, 4, 2, short, width), bf16),
            pltpu.VMEM((stages, heads, short, 2 * HD), bf16),
            pltpu.VMEM((stages, heads, short, HD), bf16),
            pltpu.VMEM((stages, heads, short, 2 * HD), bf16),
            pltpu.VMEM((stages, heads, short, HD), bf16),
            pltpu.VMEM((rows, width), bf16),
            pltpu.VMEM((rows, width), bf16),
            pltpu.VMEM((rows, width), bf16),
            pltpu.VMEM((1, 4 * width), bf16),
            pltpu.VMEM((heads, rows, HD), bf16),
            pltpu.VMEM((heads, rows, HD), bf16),
            pltpu.VMEM((short, HD), f32),
            pltpu.VMEM((short, HD), f32),
            pltpu.VMEM((stages, 2, 8, short), f32),
            pltpu.VMEM((stages, 2, 8, short), f32),
            dma((heads, 3)),
            dma((BLOCKS + 1,)),
            dma((stages, 2, PIECES)),
            dma((stages, 2, PIECES)),
            dma((stages, PIECES)),
            dma((stages, PIECES)),
            dma((stages, 2, PIECES)),
            dma((stages, 2, PIECES)),
            dma((2, stages, heads)),
            dma((2, stages, heads)),
            dma((BLOCKS, heads)),
            dma((BLOCKS, heads)),
            dma((stages, 2)),
            dma((stages, 2)),
            pltpu.SemaphoreType.REGULAR,
        ],
        compiler_params=pltpu.CompilerParams(
            collective_id=0, has_side_effects=True, vmem_limit_bytes=48 * 2**20
        ),
        cost_estimate=pl.CostEstimate(
            flops=8 * rows * depth * 3 * width, bytes_accessed=qkv_weight.size * 2, transcendentals=0
        ),
        name="relay",
    )(*(pltpu.with_memory_space_constraint(x, pltpu.HBM) for x in operands), preempted)
    return result[None, None]


def solution(mesh):
    placed = (
        P("section", "dp", None, "tensor"),
        P("section", None, "dp", "tensor"),
        P("section", None),
        P("section"),
    )
    return jax.shard_map(
        functools.partial(local, mesh.shape["section"]),
        mesh=mesh,
        in_specs=placed,
        out_specs=P("section", "dp", None, "tensor"),
        check_vma=False,
    )
```
